128 devices in a mesh: dp: 32 (over z, y_hi, x), tensor: 4 (over y_lo, core).
Axes of the slice: x: 4, y: 4 (y_hi: 2, y_lo: 2; y = y_hi * 2 + y_lo), z: 4, core: 2. Of those that a mesh axis runs over, the one named last changes fastest.
Arguments:
- acts: bfloat16 [32768, 5120], P('dp')
- grads: bfloat16 [32768, 5120], P('dp')
- eig_a: bfloat16 [5120, 5120], P('dp', 'tensor'), may hold values from -0.078125 to 0.078125
- eig_g: bfloat16 [5120, 2560], P('dp', 'tensor'), may hold values from -0.078125 to 0.078125
Outputs:
- correction: float32 [2560, 5120], P('dp', 'tensor')
The draws below stay inside these ranges and needn't reach their ends.
All inputs are finite; a program needn't handle non-finite values.
Results may differ from the reference program's by a relative error of at most 0.0003.
Values may be sent and summed in bfloat16 or wider, within the bound.
No kernel may reach another device: no remote copies, remote signals or barrier semaphores. Data moves between devices by JAX's collectives and lax.ppermute only.
A program may use at most 128 MiB of HBM per device.

```python
import math
import jax
import jax.numpy as jnp
from jax import lax

D = 5120
G_WIN = 2560
TOK_DEV = 1024
TOKENS = 32768
N_DP = 32


def scaled_rows(key, base):
    key_rows, key_cols = jax.random.split(key, 2)
    rows = jnp.exp(jax.random.uniform(key_rows, (TOKENS, 1), jnp.float32, math.log(0.3), math.log(3.0)))
    cols = jnp.exp(jax.random.uniform(key_cols, (1, D), jnp.float32, math.log(0.5), math.log(2.0)))
    return base * rows * cols


def draw_acts(key, part):
    key = jax.random.fold_in(key, 11)
    key_base, key_rest = jax.random.split(key)
    base = jax.random.normal(key_base, (TOKENS, D), jnp.float32)
    return scaled_rows(key_rest, base).astype(jnp.bfloat16)


def draw_grads(key, part):
    key = jax.random.fold_in(key, 23)
    key_base, key_rest = jax.random.split(key)
    base = jax.random.normal(key_base, (TOKENS, D), jnp.float32)
    return scaled_rows(key_rest, base).astype(jnp.bfloat16)


def levels(key, extent, shards, least, top_value):
    loudness, own = 1.0, jax.random.fold_in(key, 6)
    for position, shards_of in shards:
        steps = jnp.exp(jax.random.uniform(jax.random.fold_in(own, position), (shards_of,), jnp.float32, least / len(shards), top_value / len(shards)))
        loudness = loudness * jnp.repeat(steps, extent[position] // shards_of).reshape([-1 if axis == position else 1 for axis in range(len(extent))])
    return loudness


def centred(stream_key, shape, scale, reach, pieces=(), held_as=jnp.bfloat16):
    result = scale * jax.random.normal(stream_key, shape, jnp.float32)
    if pieces:
        result = result * levels(stream_key, shape, pieces, -0.22, 0.18)
    return jnp.clip(result, -reach, reach).astype(held_as)


def setup_inputs(seed: int = 0) -> dict:
    splits = jax.random.split(jax.random.key(seed), 5)
    return {
        "acts": draw_acts(jax.random.fold_in(splits[4], 71), 0),
        "grads": draw_grads(jax.random.fold_in(splits[4], 71), 0),
        "eig_a": centred(splits[2], (D, D), D ** -0.5, 0.078125, ((0, 32), (1, 4))),
        "eig_g": centred(splits[3], (D, G_WIN), D ** -0.5, 0.078125, ((0, 32), (1, 4))),
    }


def reference(acts, grads, eig_a, eig_g):
    blocks_a = acts.reshape(N_DP, TOK_DEV, D)
    blocks_g = grads.reshape(N_DP, TOK_DEV, D)

    def add_block(total, pair):
        block_a, block_g = pair
        proj_a = jnp.dot(block_a, eig_a, preferred_element_type=jnp.float32)
        proj_g = jnp.dot(block_g, eig_g, preferred_element_type=jnp.float32)
        sq_a = (proj_a * proj_a).astype(jnp.bfloat16)
        sq_g = (proj_g * proj_g).astype(jnp.bfloat16)
        return total + jnp.dot(sq_g.T, sq_a, preferred_element_type=jnp.float32), None

    start = jnp.zeros((G_WIN, D), jnp.float32)
    total, unused = lax.scan(add_block, start, (blocks_a, blocks_g))
    return total / jnp.float32(TOKENS)
```

```python
import functools

import jax
import jax.numpy as jnp
from jax import lax
from jax.experimental import pallas as pl
from jax.experimental.pallas import tpu as pltpu
from jax.sharding import PartitionSpec as P

AXES = ("dp", "tensor")
Z, YH, X, YL, CORE = 4, 2, 4, 2, 2
PIECE = 160
OWN = 80
TILE = 16
SHIFTS = (0, -1, 1, 2)
VMEM = 48 << 20
F32, BF16 = jnp.float32, jnp.bfloat16


def flat(z, yh, x, yl, c):
    return (((z * YH + yh) * X + x) * YL + yl) * CORE + c


def every():
    for z in range(Z):
        for yh in range(YH):
            for x in range(X):
                for yl in range(YL):
                    for c in range(CORE):
                        yield z, yh, x, yl, c


def hop(value, phase, shift):
    pairs = []
    for z, yh, x, yl, c in every():
        if (phase + c) % 2 == 0:
            to = flat(z, yh, (x + shift) % X, yl, c)
        else:
            to = flat((z + shift) % Z, yh, x, yl, c)
        pairs.append((flat(z, yh, x, yl, c), to))
    return lax.ppermute(value, AXES, pairs)


def swap(value, what):
    pairs = []
    for z, yh, x, yl, c in every():
        to = {
            "yh": flat(z, 1 - yh, x, yl, c),
            "yl": flat(z, yh, x, 1 - yl, c),
            "core": flat(z, yh, x, yl, 1 - c),
        }[what]
        pairs.append((flat(z, yh, x, yl, c), to))
    return lax.ppermute(value, AXES, pairs)


def place():
    dp = lax.axis_index("dp")
    tensor = lax.axis_index("tensor")
    return dp // (YH * X), (dp // X) % YH, dp % X, tensor // CORE, tensor % CORE


def gather(pair):
    plus, minus, far = hop(pair, 0, 1), hop(pair, 0, -1), hop(pair, 0, 2)
    block = jnp.concatenate([pair, plus, minus, far])
    half = block.shape[0] // 2
    top, bottom = block[:half], block[half:]
    plus_top = hop(top, 1, 1)
    minus_bottom = hop(bottom, 1, -1)
    plus_bottom = hop(bottom, 1, 1)
    minus_top = hop(top, 1, -1)
    far_top = hop(plus_top, 1, 1)
    far_bottom = hop(minus_bottom, 1, -1)
    return block, plus_top, plus_bottom, minus_top, minus_bottom, far_top, far_bottom


def piece_rows():
    z, yh, x, _, c = place()
    rows = []
    for outer in SHIFTS:
        for inner in SHIFTS:
            for half in range(YH):
                px = (x + jnp.where(c == 0, inner, outer)) % X
                pz = (z + jnp.where(c == 0, outer, inner)) % Z
                rows.append(((pz * YH + (yh ^ half)) * X + px) * PIECE)
    return jnp.stack(rows).astype(jnp.int32)


def project_body(transposed, rows_ref, x_ref, *refs):
    sources, out_ref, basis, sems = refs[:7], refs[7], refs[8], refs[9]
    per = 2 * len(SHIFTS)
    width = basis.shape[1]

    @pl.when(pl.program_id(0) == 0)
    def _():
        copies = []
        for outer in range(len(SHIFTS)):
            for piece in range(per):
                n = outer * per + piece
                if outer == 0:
                    source, start = sources[0], piece * PIECE
                else:
                    source = sources[2 * outer - 1 + (2 * piece // per)]
                    start = (piece % (per // 2)) * PIECE
                row = pl.multiple_of(rows_ref[n], PIECE)
                copies.append(
                    pltpu.make_async_copy(
                        source.at[pl.ds(start, PIECE)], basis.at[pl.ds(row, PIECE)], sems.at[n]
                    )
                )
        for copy in copies:
            copy.start()
        for copy in copies:
            copy.wait()

    for left in range(0, width, 256):
        right = min(left + 256, width)
        proj = jnp.dot(x_ref[...], basis[:, left:right], preferred_element_type=F32)
        square = proj * proj
        if transposed:
            out_ref[left:right, :] = square.T.astype(BF16)
        else:
            out_ref[:, left:right] = square.astype(BF16)


def project_square(x, rows, sources, transposed):
    tokens, depth = x.shape
    width = sources[0].shape[1]
    step = 256
    if transposed:
        out_shape = jax.ShapeDtypeStruct((width, tokens), BF16)
        out_spec = pl.BlockSpec((width, step), lambda i, rows: (0, i))
    else:
        out_shape = jax.ShapeDtypeStruct((tokens, width), BF16)
        out_spec = pl.BlockSpec((step, width), lambda i, rows: (i, 0))
    return pl.pallas_call(
        functools.partial(project_body, transposed),
        out_shape=out_shape,
        grid_spec=pltpu.PrefetchScalarGridSpec(
            num_scalar_prefetch=1,
            grid=(tokens // step,),
            in_specs=[pl.BlockSpec((step, depth), lambda i, rows: (i, 0))]
            + [pl.BlockSpec(memory_space=pl.ANY)] * 7,
            out_specs=out_spec,
            scratch_shapes=[pltpu.VMEM((depth, width), BF16), pltpu.SemaphoreType.DMA((32,))],
        ),
        compiler_params=pltpu.CompilerParams(
            vmem_limit_bytes=VMEM, dimension_semantics=("arbitrary",)
        ),
        cost_estimate=pl.CostEstimate(
            flops=2 * tokens * depth * width,
            bytes_accessed=2 * (tokens * depth + depth * width + tokens * width),
            transcendentals=0,
        ),
    )(rows, x, *sources)


def exponent_of(biggest):
    return jnp.clip(jnp.floor(jnp.log2(biggest)) - 14.0, -100.0, 120.0)


def encode(value, inverse):
    scaled = value * inverse
    second = scaled * scaled
    fourth = second * second
    power = fourth * fourth
    near = power.astype(BF16).astype(F32)
    return jnp.where(power < near, -near, near).astype(BF16)


def decode(code, scale):
    code = code.astype(F32)
    size = jnp.abs(code)
    power = size + code * (0.72 / 512)
    value = jnp.exp2(jnp.log2(power) * 0.125) * scale
    return jnp.where(size > 0.0, value, 0.0)


def message_scale(ref, rows):
    return jnp.exp2(ref[rows : rows + TILE, :].astype(F32)[0:1, 0:1])


def correct_body(where_ref, *refs):
    (g0, g1, g2, g3, sq_ref), outs, total = refs[:5], refs[5:9], refs[9]
    part, width = g0.shape[0], sq_ref.shape[1]
    biggest = jnp.zeros((1, 1), F32)
    for n, g_ref in enumerate((g0, g1, g2, g3)):
        start = pl.multiple_of(where_ref[n], part)
        for left in range(0, width, 256):
            block = jnp.dot(g_ref[...], sq_ref[:, left : left + 256], preferred_element_type=F32)
            total[pl.ds(start, part), left : left + 256] = block
            biggest = jnp.maximum(biggest, jnp.max(block, axis=(0, 1), keepdims=True))
    exponent = exponent_of(biggest)
    inverse = jnp.exp2(-exponent)
    for dest, out_ref in enumerate(outs):
        for sub in range(8):
            row = pl.multiple_of(where_ref[4 + dest * 8 + sub], OWN)
            block = total[pl.ds(row, OWN), :]
            at = slice(sub * OWN, (sub + 1) * OWN)
            out_ref[at, :] = block if dest == 0 else encode(block, inverse)
        if dest > 0:
            out_ref[8 * OWN :, :] = jnp.broadcast_to(exponent, (TILE, width)).astype(BF16)


def full(shape):
    return pl.BlockSpec(shape, lambda *_: (0,) * len(shape))


def correct(parts, sq, where):
    part, tokens = parts[0].shape
    width = sq.shape[1]
    rows = 8 * OWN
    shapes = [((rows, width), F32)] + [((rows + TILE, width), BF16)] * 3
    return pl.pallas_call(
        correct_body,
        out_shape=[jax.ShapeDtypeStruct(*s) for s in shapes],
        grid_spec=pltpu.PrefetchScalarGridSpec(
            num_scalar_prefetch=1,
            grid=(1,),
            in_specs=[full((part, tokens))] * 4 + [full((tokens, width))],
            out_specs=[full(s[0]) for s in shapes],
            scratch_shapes=[pltpu.VMEM((4 * part, width), F32)],
        ),
        compiler_params=pltpu.CompilerParams(vmem_limit_bytes=VMEM),
        cost_estimate=pl.CostEstimate(
            flops=8 * part * tokens * width, bytes_accessed=part * width * 16, transcendentals=0
        ),
    )(where, *parts, sq)


def add_body(split, where_ref, *refs):
    own_ref, messages, outs = refs[0], refs[1:4], refs[4:]
    rows, width = own_ref.shape
    total = refs[-1]
    outs = outs[:-1]
    scales = [message_scale(ref, rows) for ref in messages]
    biggest = jnp.zeros((1, 1), F32)
    for top in range(0, rows, OWN):
        at = slice(top, top + OWN)
        block = own_ref[at, :]
        for ref, scale in zip(messages, scales):
            block = block + decode(ref[at, :], scale)
        total[at, :] = block
        if split == 4:
            biggest = jnp.maximum(biggest, jnp.max(block, axis=(0, 1), keepdims=True))
    size = rows // split
    if split == 4:
        exponent = exponent_of(biggest)
        inverse = jnp.exp2(-exponent)
    for dest, out_ref in enumerate(outs):
        row = pl.multiple_of(where_ref[dest] * size, size)
        block = total[pl.ds(row, size), :]
        if split == 2 or dest == 0:
            out_ref[...] = block
        else:
            out_ref[:size, :] = encode(block, inverse)
            out_ref[size:, :] = jnp.broadcast_to(exponent, (TILE, width)).astype(BF16)


def add(own, messages, where, split):
    rows, width = own.shape
    size = rows // split
    if split == 4:
        shapes = [((size, width), F32)] + [((size + TILE, width), BF16)] * 3
    else:
        shapes = [((size, width), F32)] * 2
    return pl.pallas_call(
        functools.partial(add_body, split),
        out_shape=[jax.ShapeDtypeStruct(*s) for s in shapes],
        grid_spec=pltpu.PrefetchScalarGridSpec(
            num_scalar_prefetch=1,
            grid=(1,),
            in_specs=[full((rows, width))] + [full((rows + TILE, width))] * 3,
            out_specs=[full(s[0]) for s in shapes],
            scratch_shapes=[pltpu.VMEM((rows, width), F32)],
        ),
        compiler_params=pltpu.CompilerParams(vmem_limit_bytes=VMEM),
        cost_estimate=pl.CostEstimate(
            flops=rows * width * 60, bytes_accessed=rows * width * 12, transcendentals=rows * width * 6
        ),
    )(where, own, *messages)


def reduce_tables():
    z, yh, x, yl, c = place()
    tensor = yl * CORE + c
    first = [t * (8 * OWN) for t in (tensor, tensor ^ 2, tensor ^ 1, tensor ^ 3)]
    for shift in (0, 1, -1, 2):
        for q in range(4):
            for half in range(YH):
                dx = jnp.where(c == 0, (x + shift) % X, q)
                dz = jnp.where(c == 0, q, (z + shift) % Z)
                first.append(((dz * YH + half) * X + dx) * OWN)
    mine = jnp.where(c == 0, z, x)
    second = [(mine + shift) % 4 for shift in (0, 1, -1, 2)]
    third = [yh, 1 - yh]
    return [jnp.stack([jnp.asarray(v) for v in t]).astype(jnp.int32) for t in (first, second, third)]


def on_device(acts, grads, eig_a, eig_g, cuts, total_tokens):
    rows = piece_rows()
    first, second, third = reduce_tables()
    pair_g = jnp.concatenate([eig_g, swap(eig_g, "yh")])
    pair_a = jnp.concatenate([eig_a, swap(eig_a, "yh")])

    own_g = project_square(grads, rows, gather(pair_g), True)
    other_g = swap(own_g, "yl")
    parts = [own_g, other_g, swap(own_g, "core"), swap(other_g, "core")]

    results = []
    for left, right in cuts:
        sq = project_square(acts, rows, gather(pair_a[:, left:right]), False)
        own, plus, minus, far = correct(parts, sq, first)
        own, plus, minus, far = add(own, [hop(plus, 0, 1), hop(minus, 0, -1), hop(far, 0, 2)], second, 4)
        keep, send = add(own, [hop(plus, 1, 1), hop(minus, 1, -1), hop(far, 1, 2)], third, 2)
        results.append((keep + swap(send, "yh")) * (1.0 / total_tokens))
    return jnp.concatenate(results, axis=1)


def solution(mesh):
    placed = (P("dp", None), P("dp", None), P("dp", "tensor"), P("dp", "tensor"))
    body = functools.partial(on_device, cuts=((0, 768), (768, 1280)), total_tokens=32768)
    return jax.shard_map(body, mesh=mesh, in_specs=placed, out_specs=P("dp", "tensor"), check_vma=False)
```

```python
import functools

import jax
import jax.numpy as jnp
from jax import lax
from jax.experimental import pallas as pl
from jax.experimental.pallas import tpu as pltpu
from jax.sharding import PartitionSpec as P

AXES = ("dp", "tensor")
Z, YH, X, YL, CORE = 4, 2, 4, 2, 2
PIECE = 160
OWN = 80
TILE = 16
SHIFTS = (0, -1, 1, 2)
VMEM = 60 << 20
F32, BF16 = jnp.float32, jnp.bfloat16


def flat(z, yh, x, yl, c):
    return (((z * YH + yh) * X + x) * YL + yl) * CORE + c


def every():
    for z in range(Z):
        for yh in range(YH):
            for x in range(X):
                for yl in range(YL):
                    for c in range(CORE):
                        yield z, yh, x, yl, c


def hop(value, phase, shift):
    pairs = []
    for z, yh, x, yl, c in every():
        if (phase + c) % 2 == 0:
            to = flat(z, yh, (x + shift) % X, yl, c)
        else:
            to = flat((z + shift) % Z, yh, x, yl, c)
        pairs.append((flat(z, yh, x, yl, c), to))
    return lax.ppermute(value, AXES, pairs)


def swap(value, what):
    pairs = []
    for z, yh, x, yl, c in every():
        to = {
            "yh": flat(z, 1 - yh, x, yl, c),
            "yl": flat(z, yh, x, 1 - yl, c),
            "mirror": flat(z, 1 - yh, x, 1 - yl, c),
            "core": flat(z, yh, x, yl, 1 - c),
        }[what]
        pairs.append((flat(z, yh, x, yl, c), to))
    return lax.ppermute(value, AXES, pairs)


def place():
    dp = lax.axis_index("dp")
    tensor = lax.axis_index("tensor")
    return dp // (YH * X), (dp // X) % YH, dp % X, tensor // CORE, tensor % CORE


def after(value, *earlier):
    return lax.optimization_barrier((value, *earlier))[0]


def gather_narrow(pair):
    return [pair, hop(pair, 0, 1), hop(pair, 0, -1), hop(pair, 0, 2)]


def gather_wide(narrow):
    block = jnp.concatenate(narrow)
    return [block, hop(block, 1, 1), hop(block, 1, -1)]


def gather_far(wide):
    half = wide[0].shape[0] // 2
    return [*wide, hop(wide[1][:half], 1, 1), hop(wide[2][half:], 1, -1)]


def piece_rows():
    z, yh, x, _, c = place()
    rows = []
    for outer in SHIFTS:
        for inner in SHIFTS:
            for half in range(YH):
                px = (x + jnp.where(c == 0, inner, outer)) % X
                pz = (z + jnp.where(c == 0, outer, inner)) % Z
                rows.append(((pz * YH + (yh ^ half)) * X + px) * PIECE)
    return jnp.stack(rows).astype(jnp.int32)


def load_basis(rows_ref, sources, basis, sems):
    copies = []
    for source in sources:
        for start in range(0, source.shape[0], PIECE):
            n = len(copies)
            row = pl.multiple_of(rows_ref[n], PIECE)
            copies.append(
                pltpu.make_async_copy(
                    source.at[pl.ds(start, PIECE)], basis.at[pl.ds(row, PIECE)], sems.at[n]
                )
            )
    for copy in copies:
        copy.start()
    for copy in copies:
        copy.wait()


def squares(x, basis, out_ref, transposed):
    width = basis.shape[1]
    for left in range(0, width, 256):
        right = min(left + 256, width)
        proj = jnp.dot(x, basis[:, left:right], preferred_element_type=F32)
        square = proj * proj
        if transposed:
            out_ref[left:right, :] = square.T.astype(BF16)
        else:
            out_ref[:, left:right] = square.astype(BF16)


def project_body(count, transposed, rows_ref, first_ref, x_ref, *refs):
    sources, (out_ref, basis, sems) = refs[:count], refs[count:]

    @pl.when(pl.program_id(0) == 0)
    def _():
        load_basis(rows_ref, sources, basis, sems)

    squares(x_ref[...], basis, out_ref, transposed)


def project_cost(tokens, depth, width):
    return pl.CostEstimate(
        flops=2 * tokens * depth * width,
        bytes_accessed=2 * (tokens * depth + depth * width + tokens * width),
        transcendentals=0,
    )


def project_square(x, shard, tokens, rows, sources, transposed):
    depth = x.shape[1]
    width = sources[0].shape[1]
    step = 256
    first = jnp.reshape(shard * (tokens // step), (1,)).astype(jnp.int32)
    if transposed:
        out_shape = jax.ShapeDtypeStruct((width, tokens), BF16)
        out_spec = pl.BlockSpec((width, step), lambda i, rows, first: (0, i))
    else:
        out_shape = jax.ShapeDtypeStruct((tokens, width), BF16)
        out_spec = pl.BlockSpec((step, width), lambda i, rows, first: (i, 0))
    return pl.pallas_call(
        functools.partial(project_body, len(sources), transposed),
        out_shape=out_shape,
        grid_spec=pltpu.PrefetchScalarGridSpec(
            num_scalar_prefetch=2,
            grid=(tokens // step,),
            in_specs=[pl.BlockSpec((step, depth), lambda i, rows, first: (first[0] + i, 0))]
            + [pl.BlockSpec(memory_space=pl.ANY)] * len(sources),
            out_specs=out_spec,
            scratch_shapes=[pltpu.VMEM((depth, width), BF16), pltpu.SemaphoreType.DMA((32,))],
        ),
        compiler_params=pltpu.CompilerParams(
            vmem_limit_bytes=VMEM, dimension_semantics=("arbitrary",)
        ),
        cost_estimate=project_cost(tokens, depth, width),
    )(rows, first, x, *sources)


def exponent_of(biggest):
    return jnp.clip(jnp.floor(jnp.log2(biggest)) - 14.0, -100.0, 120.0)


def encode(value, inverse):
    scaled = value * inverse
    second = scaled * scaled
    fourth = second * second
    power = fourth * fourth
    near = power.astype(BF16).astype(F32)
    return jnp.where(power < near, -near, near).astype(BF16)


def decode(code, scale):
    code = code.astype(F32)
    size = jnp.abs(code)
    power = size + code * (0.72 / 512)
    value = jnp.exp2(jnp.log2(power) * 0.125) * scale
    return jnp.where(size > 0.0, value, 0.0)


def message_scale(ref, rows):
    return jnp.exp2(ref[rows : rows + TILE, :].astype(F32)[0:1, 0:1])


def near_body(cuts, where_ref, *refs):
    near, sq_ref, outs = refs[:4], refs[4], refs[5:]
    part = near[0].shape[0]
    for n in range(4):
        start = pl.multiple_of(where_ref[n], part)
        for (left, right), out_ref in zip(cuts, outs):
            for low in range(left, right, 256):
                high = min(low + 256, right)
                block = jnp.dot(near[n][...], sq_ref[:, low:high], preferred_element_type=F32)
                out_ref[pl.ds(start, part), low - left : high - left] = block


def correct_body(left, where_ref, *refs):
    far, (sq_ref, near_ref), outs, total = refs[:4], refs[4:6], refs[6:10], refs[10]
    part, width = far[0].shape[0], near_ref.shape[1]
    biggest = jnp.zeros((1, 1), F32)
    for n in range(4):
        start = pl.multiple_of(where_ref[n], part)
        for low in range(0, width, 256):
            high = min(low + 256, width)
            block = jnp.dot(far[n][...], sq_ref[:, left + low : left + high], preferred_element_type=F32)
            block += near_ref[pl.ds(start, part), low:high]
            total[pl.ds(start, part), low:high] = block
            biggest = jnp.maximum(biggest, jnp.max(block, axis=(0, 1), keepdims=True))
    exponent = exponent_of(biggest)
    inverse = jnp.exp2(-exponent)
    for dest, out_ref in enumerate(outs):
        for sub in range(8):
            row = pl.multiple_of(where_ref[4 + dest * 8 + sub], OWN)
            block = total[pl.ds(row, OWN), :]
            at = slice(sub * OWN, (sub + 1) * OWN)
            out_ref[at, :] = block if dest == 0 else encode(block, inverse)
        if dest > 0:
            out_ref[8 * OWN :, :] = jnp.broadcast_to(exponent, (TILE, width)).astype(BF16)


def full(shape):
    return pl.BlockSpec(shape, lambda *_: (0,) * len(shape))


def correct_cost(part, tokens, width):
    return pl.CostEstimate(
        flops=8 * part * tokens * width, bytes_accessed=part * (8 * tokens + 16 * width), transcendentals=0
    )


def correct_near(near, sq, where, cuts):
    part, tokens = near[0].shape
    shapes = [(4 * part, right - left) for left, right in cuts]
    return pl.pallas_call(
        functools.partial(near_body, cuts),
        out_shape=[jax.ShapeDtypeStruct(shape, F32) for shape in shapes],
        grid_spec=pltpu.PrefetchScalarGridSpec(
            num_scalar_prefetch=1,
            grid=(1,),
            in_specs=[full((part, tokens))] * 4 + [full(sq.shape)],
            out_specs=[full(shape) for shape in shapes],
        ),
        compiler_params=pltpu.CompilerParams(vmem_limit_bytes=VMEM),
        cost_estimate=correct_cost(part, tokens, sq.shape[1]),
    )(where, *near, sq)


def correct(far, sq, near_sum, where, left):
    part, tokens = far[0].shape
    width = near_sum.shape[1]
    rows = 8 * OWN
    shapes = [((rows, width), F32)] + [((rows + TILE, width), BF16)] * 3
    return pl.pallas_call(
        functools.partial(correct_body, left),
        out_shape=[jax.ShapeDtypeStruct(*s) for s in shapes],
        grid_spec=pltpu.PrefetchScalarGridSpec(
            num_scalar_prefetch=1,
            grid=(1,),
            in_specs=[full((part, tokens))] * 4 + [full(sq.shape), full(near_sum.shape)],
            out_specs=[full(s[0]) for s in shapes],
            scratch_shapes=[pltpu.VMEM((4 * part, width), F32)],
        ),
        compiler_params=pltpu.CompilerParams(vmem_limit_bytes=VMEM),
        cost_estimate=correct_cost(part, tokens, width),
    )(where, *far, sq, near_sum)


def add_body(split, factor, where_ref, *refs):
    own_ref, messages, outs = refs[0], refs[1:4], refs[4:]
    rows, width = own_ref.shape
    total = refs[-1]
    outs = outs[:-1]
    scales = [message_scale(ref, rows) for ref in messages]
    biggest = jnp.zeros((1, 1), F32)
    for top in range(0, rows, OWN):
        at = slice(top, top + OWN)
        block = own_ref[at, :]
        for ref, scale in zip(messages, scales):
            block = block + decode(ref[at, :], scale)
        total[at, :] = block
        if split == 4:
            biggest = jnp.maximum(biggest, jnp.max(block, axis=(0, 1), keepdims=True))
    size = rows // split
    if split == 4:
        exponent = exponent_of(biggest)
        inverse = jnp.exp2(-exponent)
    for dest, out_ref in enumerate(outs):
        row = pl.multiple_of(where_ref[dest] * size, size)
        block = total[pl.ds(row, size), :]
        if split == 2 or dest == 0:
            out_ref[...] = block * factor
        else:
            out_ref[:size, :] = encode(block, inverse)
            out_ref[size:, :] = jnp.broadcast_to(exponent, (TILE, width)).astype(BF16)


def add(own, messages, where, split, factor):
    rows, width = own.shape
    size = rows // split
    if split == 4:
        shapes = [((size, width), F32)] + [((size + TILE, width), BF16)] * 3
    else:
        shapes = [((size, width), F32)] * 2
    return pl.pallas_call(
        functools.partial(add_body, split, factor),
        out_shape=[jax.ShapeDtypeStruct(*s) for s in shapes],
        grid_spec=pltpu.PrefetchScalarGridSpec(
            num_scalar_prefetch=1,
            grid=(1,),
            in_specs=[full((rows, width))] + [full((rows + TILE, width))] * 3,
            out_specs=[full(s[0]) for s in shapes],
            scratch_shapes=[pltpu.VMEM((rows, width), F32)],
        ),
        compiler_params=pltpu.CompilerParams(vmem_limit_bytes=VMEM),
        cost_estimate=pl.CostEstimate(
            flops=rows * width * 60, bytes_accessed=rows * width * 12, transcendentals=rows * width * 6
        ),
    )(where, own, *messages)


def reduce_tables():
    z, yh, x, yl, c = place()
    tensor = yl * CORE + c
    first = [t * (8 * OWN) for t in (tensor, tensor ^ 2, tensor ^ 1, tensor ^ 3)]
    for shift in (0, 1, -1, 2):
        for q in range(4):
            for half in range(YH):
                dx = jnp.where(c == 0, (x + shift) % X, q)
                dz = jnp.where(c == 0, q, (z + shift) % Z)
                first.append(((dz * YH + half) * X + dx) * OWN)
    mine = jnp.where(c == 0, z, x)
    second = [(mine + shift) % 4 for shift in (0, 1, -1, 2)]
    third = [yh, 1 - yh]
    return [jnp.stack([jnp.asarray(v) for v in t]).astype(jnp.int32) for t in (first, second, third)]


def share_tokens(acts):
    _, _, _, yl, c = place()
    quarter = acts.shape[0] // 4
    mine = lax.dynamic_slice(acts, ((yl * CORE + c) * quarter, 0), (quarter, acts.shape[1]))
    lines = [
        [flat(z, yh, x, yl, c) for yh in range(YH) for yl in range(YL) for c in range(CORE)]
        for z in range(Z)
        for x in range(X)
    ]
    return lax.all_gather(mine, AXES, axis_index_groups=lines, axis=0, tiled=True)


def share_squares(own, other_core, before_diagonal, before_last):
    half = own.shape[0] // 2
    beside, across = swap(own, "yl"), swap(own, "mirror")
    near = [own, beside, other_core, swap(beside, "core")]
    other_across = swap(across, "core")
    beside, across = after(beside, before_diagonal), after(across, before_diagonal)
    one, other = swap(beside[:half], "mirror"), swap(across[half:], "yl")
    diagonal = jnp.concatenate([after(one, before_last), after(other, before_last)])
    return near, [diagonal, across, swap(diagonal, "core"), other_across]


def on_device(acts, grads, eig_a, eig_g, cuts, total_tokens):
    first, second, third = reduce_tables()
    _, yh, _, _, _ = place()
    half = eig_a.shape[1] // 2
    other_g = swap(eig_g, "yh")
    low, high = eig_a[:, :half], eig_a[:, half:]
    other_a = swap(after(jnp.where(yh == 0, high, low), other_g), "yh")
    line = share_tokens(acts)
    tokens = acts.shape[0]
    rows = piece_rows()

    narrow_g = gather_narrow(jnp.concatenate([eig_g, other_g]))
    narrow_g[0] = after(narrow_g[0], other_a)
    wide_g = gather_wide(narrow_g)
    basis_g = gather_far(wide_g)

    pair_a = jnp.concatenate([jnp.where(yh == 0, low, high), other_a])
    narrow_a = gather_narrow(after(pair_a, *wide_g))
    narrow_a[0] = after(narrow_a[0], *basis_g)
    wide_a = gather_wide(narrow_a)
    own_g = project_square(grads, jnp.int32(0), tokens, rows, basis_g, True)
    own_g_other_core = swap(own_g, "core")
    wide_a[1:] = [after(v, own_g_other_core) for v in wide_a[1:]]
    basis_a = gather_far(wide_a)
    sq_near = project_square(acts, jnp.int32(0), tokens, rows, basis_a, False)
    sq_far = project_square(line, 1 - yh, tokens, rows, basis_a, False)
    near, far = share_squares(own_g, own_g_other_core, sq_near, sq_far)

    near_sums = correct_near(near, after(sq_near, sq_far), first, cuts)
    results, held = [], ()
    for (left, _), near_sum in zip(cuts, near_sums):
        own, *messages = correct(far, sq_far, near_sum, first, left)
        messages = [after(message, *held) for message in messages]
        held = [hop(message, 0, shift) for message, shift in zip(messages, (1, -1, 2))]
        own, *messages = add(own, held, second, 4, 1.0)
        messages = [hop(message, 1, shift) for message, shift in zip(messages, (1, -1, 2))]
        results.append(add(own, messages, third, 2, 1.0 / total_tokens))
    keep = jnp.concatenate([r[0] for r in results], axis=1)
    got = jnp.concatenate([swap(r[1], "yh") for r in results], axis=1)
    return jnp.where(yh == 0, jnp.concatenate([keep, got], axis=1), jnp.concatenate([got, keep], axis=1))


def solution(mesh):
    placed = (P("dp", None), P("dp", None), P("dp", "tensor"), P("dp", "tensor"))
    body = functools.partial(on_device, cuts=((0, 384), (384, 640)), total_tokens=32768)
    return jax.shard_map(body, mesh=mesh, in_specs=placed, out_specs=P("dp", "tensor"), check_vma=False)
```

```python
import functools

import jax
import jax.numpy as jnp
from jax import lax
from jax.experimental import pallas as pl
from jax.experimental.pallas import tpu as pltpu
from jax.sharding import PartitionSpec as P

AXES = ("dp", "tensor")
Z, YH, X, YL, CORE = 4, 2, 4, 2, 2
PIECE = 160
OWN = 80
TILE = 16
SHIFTS = (0, -1, 1, 2)
VMEM = 60 << 20
F32, BF16 = jnp.float32, jnp.bfloat16


def flat(z, yh, x, yl, c):
    return (((z * YH + yh) * X + x) * YL + yl) * CORE + c


def every():
    for z in range(Z):
        for yh in range(YH):
            for x in range(X):
                for yl in range(YL):
                    for c in range(CORE):
                        yield z, yh, x, yl, c


def hop(value, phase, shift, flip=0):
    pairs = []
    for z, yh, x, yl, c in every():
        if (phase + c) % 2 == 0:
            to = flat(z, yh ^ flip, (x + shift) % X, yl, c)
        else:
            to = flat((z + shift) % Z, yh ^ flip, x, yl, c)
        pairs.append((flat(z, yh, x, yl, c), to))
    return lax.ppermute(value, AXES, pairs)


def swap(value, what):
    pairs = []
    for z, yh, x, yl, c in every():
        to = {
            "yh": flat(z, 1 - yh, x, yl, c),
            "yl": flat(z, yh, x, 1 - yl, c),
            "mirror": flat(z, 1 - yh, x, 1 - yl, c),
            "core": flat(z, yh, x, yl, 1 - c),
        }[what]
        pairs.append((flat(z, yh, x, yl, c), to))
    return lax.ppermute(value, AXES, pairs)


def place():
    dp = lax.axis_index("dp")
    tensor = lax.axis_index("tensor")
    return dp // (YH * X), (dp // X) % YH, dp % X, tensor // CORE, tensor % CORE


def after(value, *earlier):
    return lax.optimization_barrier((value, *earlier))[0]


def gather_narrow(pair):
    return [pair, hop(pair, 0, 1), hop(pair, 0, -1), hop(pair, 0, 2)]


def gather_wide(narrow, earlier=()):
    top, bottom = jnp.concatenate(narrow[:2]), jnp.concatenate(narrow[2:])
    top, bottom = after(top, *earlier), after(bottom, *earlier)
    return [top, bottom, hop(top, 1, 1), hop(bottom, 1, 1), hop(top, 1, -1), hop(bottom, 1, -1)]


def gather_wide_whole(narrow, earlier=()):
    block = after(jnp.concatenate(narrow), *earlier)
    return [block, hop(block, 1, 1), hop(block, 1, -1)]


def gather_far(wide, *earlier):
    if len(wide) == 3:
        half = wide[0].shape[0] // 2
        plus, minus = after(wide[1], *earlier)[:half], after(wide[2], *earlier)[half:]
    else:
        plus, minus = after(wide[2], *earlier), after(wide[5], *earlier)
    return [*wide, hop(plus, 1, 1), hop(minus, 1, -1)]


def piece_rows():
    z, yh, x, _, c = place()
    rows = []
    for outer in SHIFTS:
        for inner in SHIFTS:
            for half in range(YH):
                px = (x + jnp.where(c == 0, inner, outer)) % X
                pz = (z + jnp.where(c == 0, outer, inner)) % Z
                rows.append(((pz * YH + (yh ^ half)) * X + px) * PIECE)
    return jnp.stack(rows).astype(jnp.int32)


def locate(sources, piece):
    for source in sources:
        held = source.shape[0] // PIECE
        if piece < held:
            return source, piece
        piece -= held


def project_body(transposed, rows_ref, place_ref, x_ref, *refs):
    *sources, out_ref, basis, total, sems = refs
    width, depth = basis.shape[1], basis.shape[0] // 4

    def start(chunk):
        for core in range(CORE):
            @pl.when(place_ref[1] == core)
            def _():
                for other in range(4):
                    outer, inner = (chunk, other) if core == 0 else (other, chunk)
                    for half in range(YH):
                        row = pl.multiple_of(rows_ref[outer * 8 + inner * 2 + half], PIECE)
                        source, piece = locate(sources, outer * 8 + inner * 2 + half)
                        pltpu.make_async_copy(
                            source.at[pl.ds(piece * PIECE, PIECE)],
                            basis.at[pl.ds(row, PIECE)],
                            sems.at[chunk],
                        ).start()

    def store(at, proj):
        if transposed:
            out_ref[at, :] = (proj * proj).T.astype(BF16)
        else:
            out_ref[:, at] = (proj * proj).astype(BF16)

    parts = [slice(left, min(left + 256, width)) for left in range(0, width, 256)]

    @pl.when(pl.program_id(0) == 0)
    def _():
        start(0)
        start(1)
        for chunk in range(4):
            pltpu.make_async_copy(basis.at[pl.ds(0, depth)], basis.at[pl.ds(0, depth)], sems.at[chunk]).wait()
            if chunk + 2 < 4:
                start(chunk + 2)
            rows = pl.ds(pl.multiple_of(place_ref[2 + chunk], depth), depth)
            for at in parts:
                proj = jnp.dot(x_ref[:, rows], basis[rows, at], preferred_element_type=F32)
                if chunk > 0:
                    proj += total[:, at]
                if chunk < 3:
                    total[:, at] = proj
                else:
                    store(at, proj)

    @pl.when(pl.program_id(0) > 0)
    def _():
        for at in parts:
            store(at, jnp.dot(x_ref[...], basis[:, at], preferred_element_type=F32))


def project_cost(tokens, depth, width):
    return pl.CostEstimate(
        flops=2 * tokens * depth * width // 20,
        bytes_accessed=2 * (tokens * depth + depth * width + tokens * width) // 20,
        transcendentals=0,
    )


def project_square(x, shard, tokens, rows, sources, transposed):
    depth = x.shape[1]
    width = sources[0].shape[1]
    step = 256
    z, _, _, _, c = place()
    table = [shard * (tokens // step), c, *(((z + shift) % Z) * (depth // Z) for shift in SHIFTS)]
    first = jnp.stack(table).astype(jnp.int32)
    if transposed:
        out_shape = jax.ShapeDtypeStruct((width, tokens), BF16)
        out_spec = pl.BlockSpec((width, step), lambda i, rows, first: (0, i))
    else:
        out_shape = jax.ShapeDtypeStruct((tokens, width), BF16)
        out_spec = pl.BlockSpec((step, width), lambda i, rows, first: (i, 0))
    return pl.pallas_call(
        functools.partial(project_body, transposed),
        out_shape=out_shape,
        grid_spec=pltpu.PrefetchScalarGridSpec(
            num_scalar_prefetch=2,
            grid=(tokens // step,),
            in_specs=[pl.BlockSpec((step, depth), lambda i, rows, first: (first[0] + i, 0))]
            + [pl.BlockSpec(memory_space=pl.ANY)] * len(sources),
            out_specs=out_spec,
            scratch_shapes=[
                pltpu.VMEM((depth, width), BF16),
                pltpu.VMEM((step, width), F32),
                pltpu.SemaphoreType.DMA((4,)),
            ],
        ),
        compiler_params=pltpu.CompilerParams(
            vmem_limit_bytes=VMEM, dimension_semantics=("arbitrary",)
        ),
        cost_estimate=project_cost(tokens, depth, width),
    )(rows, first, x, *sources)


def exponent_of(biggest):
    return jnp.clip(jnp.floor(jnp.log2(biggest)) - 14.0, -100.0, 120.0)


def encode(value, inverse):
    scaled = value * inverse
    second = scaled * scaled
    fourth = second * second
    power = fourth * fourth
    near = power.astype(BF16).astype(F32)
    return jnp.where(power < near, -near, near).astype(BF16)


def decode(code, scale):
    code = code.astype(F32)
    size = jnp.abs(code)
    power = size + code * (0.72 / 512)
    value = jnp.exp2(jnp.log2(power) * 0.125) * scale
    return jnp.where(size > 0.0, value, 0.0)


def message_scale(ref, rows):
    return jnp.exp2(ref[rows : rows + TILE, :].astype(F32)[0:1, 0:1])


def correct_body(where_ref, *refs):
    parts, squares, outs = refs[:8], refs[8:10], refs[10:14]
    held_parts, held_squares, total, own, codes, sems = refs[14:]
    part, width = own.shape
    loads = []
    for side in range(2):
        loads.append(pltpu.make_async_copy(squares[side], held_squares.at[side], sems.at[5 * side]))
        for n in range(4):
            source = parts[side * 4 + n]
            if source.shape[0] > part:
                source = source.at[pl.ds(pl.multiple_of(where_ref[20], part), part)]
            rows = pl.ds(pl.multiple_of(where_ref[n], part), part)
            loads.append(pltpu.make_async_copy(source, held_parts.at[side, rows], sems.at[5 * side + 1 + n]))
    for load in loads:
        load.start()
    biggest = jnp.zeros((1, 1), F32)
    for side in range(2):
        for load in loads[5 * side : 5 * side + 5]:
            load.wait()
        for low in range(0, width, 256):
            at = slice(low, min(low + 256, width))
            block = jnp.dot(held_parts[side], held_squares[side, :, at], preferred_element_type=F32)
            if side == 1:
                block += total[:, at]
                biggest = jnp.maximum(biggest, jnp.max(block, axis=(0, 1), keepdims=True))
            total[:, at] = block
    exponent = exponent_of(biggest)
    inverse = jnp.exp2(-exponent)
    stores = []
    for dest in (3, 1, 2, 0):
        for sub in range(4):
            row = pl.multiple_of(where_ref[4 + dest * 4 + sub], OWN)
            block = total[pl.ds(row, OWN), :]
            at = slice(sub * OWN, (sub + 1) * OWN)
            if dest == 0:
                own[at, :] = block
            else:
                codes[dest - 1, at, :] = encode(block, inverse)
        if dest > 0:
            codes[dest - 1, 4 * OWN :, :] = jnp.broadcast_to(exponent, (TILE, width)).astype(BF16)
        source = own if dest == 0 else codes.at[dest - 1]
        stores.append(pltpu.make_async_copy(source, outs[dest], sems.at[10 + dest]))
        stores[-1].start()
    for store in stores:
        store.wait()


def full(shape):
    return pl.BlockSpec(shape, lambda *_: (0,) * len(shape))


def correct(near, far, sq_near, sq_far, where):
    tokens, width = sq_near.shape
    rows = 4 * OWN
    shapes = [((rows, width), F32)] + [((rows + TILE, width), BF16)] * 3
    return pl.pallas_call(
        correct_body,
        out_shape=[jax.ShapeDtypeStruct(*s) for s in shapes],
        grid_spec=pltpu.PrefetchScalarGridSpec(
            num_scalar_prefetch=1,
            grid=(1,),
            in_specs=[pl.BlockSpec(memory_space=pl.ANY)] * 10,
            out_specs=[pl.BlockSpec(memory_space=pl.ANY)] * 4,
            scratch_shapes=[
                pltpu.VMEM((2, 4 * rows, tokens), BF16),
                pltpu.VMEM((2, tokens, width), BF16),
                pltpu.VMEM((4 * rows, width), F32),
                pltpu.VMEM((rows, width), F32),
                pltpu.VMEM((3, rows + TILE, width), BF16),
                pltpu.SemaphoreType.DMA((14,)),
            ],
        ),
        compiler_params=pltpu.CompilerParams(vmem_limit_bytes=VMEM),
        cost_estimate=pl.CostEstimate(flops=rows * tokens * width, bytes_accessed=rows * tokens, transcendentals=0),
    )(where, *near, *far, sq_near, sq_far)


def add_body(where_ref, own_ref, plus_ref, minus_ref, away_ref, *refs):
    outs, total = refs[:4], refs[4]
    rows, width = own_ref.shape
    messages = (plus_ref, minus_ref, away_ref)
    scales = [message_scale(ref, rows) for ref in messages]
    biggest = jnp.zeros((1, 1), F32)
    for top in range(0, rows, OWN):
        at = slice(top, top + OWN)
        block = own_ref[at, :]
        for ref, scale in zip(messages, scales):
            block = block + decode(ref[at, :], scale)
        total[at, :] = block
        biggest = jnp.maximum(biggest, jnp.max(block, axis=(0, 1), keepdims=True))
    exponent = exponent_of(biggest)
    inverse = jnp.exp2(-exponent)
    for n, out_ref in enumerate(outs):
        block = total[pl.ds(pl.multiple_of(where_ref[n], OWN), OWN), :]
        if out_ref.shape[0] == OWN:
            out_ref[...] = block
        else:
            out_ref[:OWN, :] = encode(block, inverse)
            out_ref[OWN:, :] = jnp.broadcast_to(exponent, (TILE, width)).astype(BF16)


def add(own, messages, where, keep):
    rows, width = own.shape
    shapes = [((OWN, width), F32) if keep else ((OWN + TILE, width), BF16)] + [((OWN + TILE, width), BF16)] * 3
    return pl.pallas_call(
        add_body,
        out_shape=[jax.ShapeDtypeStruct(*s) for s in shapes],
        grid_spec=pltpu.PrefetchScalarGridSpec(
            num_scalar_prefetch=1,
            grid=(1,),
            in_specs=[full((rows, width))] + [full((rows + TILE, width))] * 3,
            out_specs=[full(s[0]) for s in shapes],
            scratch_shapes=[pltpu.VMEM((rows, width), F32)],
        ),
        compiler_params=pltpu.CompilerParams(vmem_limit_bytes=VMEM),
        cost_estimate=pl.CostEstimate(flops=rows * width, bytes_accessed=rows * width, transcendentals=0),
    )(where, own, *messages)


def finish_body(factor, where_ref, own_ref, *refs):
    codes, out_ref = refs[:7], refs[7]
    width = own_ref.shape[1]
    for side in range(YH):
        total = own_ref[...] if side == 0 else jnp.zeros((OWN, width), F32)
        for ref in codes[3 * side : 3 + 4 * side]:
            total = total + decode(ref[:OWN, :], message_scale(ref, OWN))
        out_ref[:, pl.ds(pl.multiple_of(where_ref[side], width), width)] = total * factor


def finish(own, codes, where, factor):
    width = own.shape[1]
    return pl.pallas_call(
        functools.partial(finish_body, factor),
        out_shape=jax.ShapeDtypeStruct((OWN, YH * width), F32),
        grid_spec=pltpu.PrefetchScalarGridSpec(
            num_scalar_prefetch=1,
            grid=(1,),
            in_specs=[full(own.shape)] + [full((OWN + TILE, width))] * 7,
            out_specs=full((OWN, YH * width)),
        ),
        compiler_params=pltpu.CompilerParams(vmem_limit_bytes=VMEM),
        cost_estimate=pl.CostEstimate(flops=OWN * width, bytes_accessed=OWN * width, transcendentals=0),
    )(where, own, *codes)


def tables(flip):
    z, yh, x, yl, c = place()
    tensor = yl * CORE + c
    rows = 4 * OWN
    first = [t * rows for t in (tensor, tensor ^ 2, tensor ^ 1, tensor ^ 3)]
    for shift in (0, 1, -1, 2):
        for q in range(4):
            first.append(jnp.where(c == 0, q * rows + (x + shift) % X * OWN, (z + shift) % Z * rows + q * OWN))
    first.append((yh ^ flip) * rows)
    mine = jnp.where(c == 0, z, x)
    second = [(mine + shift) % 4 * OWN for shift in (0, 1, -1, 2)]
    return [jnp.stack([jnp.asarray(v) for v in t]).astype(jnp.int32) for t in (first, second)]


def share_tokens(acts):
    _, _, _, yl, c = place()
    quarter = acts.shape[0] // 4
    mine = lax.dynamic_slice(acts, ((yl * CORE + c) * quarter, 0), (quarter, acts.shape[1]))
    lines = [
        [flat(z, yh, x, yl, c) for yh in range(YH) for yl in range(YL) for c in range(CORE)]
        for z in range(Z)
        for x in range(X)
    ]
    return lax.all_gather(mine, AXES, axis_index_groups=lines, axis=0, tiled=True)


def on_device(acts, grads, eig_a, eig_g, total_tokens):
    _, yh, _, _, _ = place()
    half = eig_a.shape[1] // 2
    low, high = eig_a[:, :half], eig_a[:, half:]
    split = eig_g.shape[1]
    line = share_tokens(acts)
    tokens = acts.shape[0]
    rows = piece_rows()

    other = swap(jnp.concatenate([eig_g, jnp.where(yh == 0, high, low)], axis=1), "yh")
    pair = jnp.concatenate([jnp.concatenate([eig_g, jnp.where(yh == 0, low, high)], axis=1), other])
    narrow = gather_narrow(pair)
    wide_g = gather_wide([v[:, :split] for v in narrow])
    basis_g = gather_far(wide_g)
    wide_a = gather_wide_whole([v[:, split:] for v in narrow], (wide_g[2], wide_g[5]))
    own_g = project_square(grads, jnp.int32(0), tokens, rows, basis_g, True)
    own_g_other_core = swap(own_g, "core")
    basis_a = gather_far(wide_a, own_g_other_core)
    sq_near = project_square(acts, jnp.int32(0), tokens, rows, basis_a, False)
    sq_far = project_square(line, 1 - yh, tokens, rows, basis_a, False)
    rows = own_g.shape[0] // 2
    given = lax.dynamic_slice(own_g, ((1 - yh) * rows, 0), (rows, tokens))
    kept = lax.dynamic_slice(own_g, (yh * rows, 0), (rows, tokens))
    beside_given, across_kept = swap(given, "yl"), swap(kept, "mirror")
    beside_given, across_kept = after(beside_given, sq_near), after(across_kept, sq_near)
    diagonal_kept = swap(across_kept, "yl")
    kept, given, beside = after(kept, across_kept), after(given, beside_given), beside_given
    beside_kept, across_given = swap(kept, "yl"), swap(given, "mirror")
    diagonal_given = swap(beside, "mirror")

    diagonal_kept = after(diagonal_kept, sq_far, across_given)
    near = [own_g, beside_given, own_g_other_core, swap(beside_given, "core")]
    far = [diagonal_kept, across_kept, swap(diagonal_kept, "core"), swap(across_kept, "core")]
    first, second = tables(1)
    shifts = (1, -1, 2)
    own, *messages = correct(near, far, sq_near, sq_far, first)
    beside_kept, diagonal_given = after(beside_kept, own), after(diagonal_given, own)
    near = [own_g, beside_kept, own_g_other_core, swap(beside_kept, "core")]
    far = [diagonal_given, across_given, swap(diagonal_given, "core"), swap(across_given, "core")]
    received = [hop(message, 0, shift) for message, shift in zip(messages, shifts)]
    first, _ = tables(0)
    kept_own, *kept_messages = correct(near, far, sq_near, sq_far, first)
    given_codes = add(after(own, kept_own), received, second, False)
    kept_messages = [after(message, *received) for message in kept_messages]
    received = [hop(message, 0, shift) for message, shift in zip(kept_messages, shifts)]
    given_codes = [hop(code, 1, shift, 1) for code, shift in zip(given_codes, (0, *shifts))]
    own, *codes = add(kept_own, received, second, True)
    codes = [hop(code, 1, shift) for code, shift in zip(codes, shifts)]
    columns = jnp.stack([yh, 1 - yh]).astype(jnp.int32) * own.shape[1]
    return finish(own, codes + given_codes, columns, 1.0 / total_tokens)


def solution(mesh):
    placed = (P("dp", None), P("dp", None), P("dp", "tensor"), P("dp", "tensor"))
    body = functools.partial(on_device, total_tokens=32768)
    return jax.shard_map(body, mesh=mesh, in_specs=placed, out_specs=P("dp", "tensor"), check_vma=False)
```

```python
import functools

import jax
import jax.numpy as jnp
from jax import lax
from jax.experimental import pallas as pl
from jax.experimental.pallas import tpu as pltpu
from jax.sharding import PartitionSpec as P

AXES = ("dp", "tensor")
Z, YH, X, YL, CORE = 4, 2, 4, 2, 2
PIECE = 160
OWN = 80
TILE = 16
SHIFTS = (0, -1, 1, 2)
VMEM = 60 << 20
F32, BF16 = jnp.float32, jnp.bfloat16


def flat(z, yh, x, yl, c):
    return (((z * YH + yh) * X + x) * YL + yl) * CORE + c


def every():
    for z in range(Z):
        for yh in range(YH):
            for x in range(X):
                for yl in range(YL):
                    for c in range(CORE):
                        yield z, yh, x, yl, c


def hop(value, phase, shift, flip=0):
    pairs = []
    for z, yh, x, yl, c in every():
        if (phase + c) % 2 == 0:
            to = flat(z, yh ^ flip, (x + shift) % X, yl, c)
        else:
            to = flat((z + shift) % Z, yh ^ flip, x, yl, c)
        pairs.append((flat(z, yh, x, yl, c), to))
    return lax.ppermute(value, AXES, pairs)


def swap(value, what):
    pairs = []
    for z, yh, x, yl, c in every():
        to = {
            "yh": flat(z, 1 - yh, x, yl, c),
            "yl": flat(z, yh, x, 1 - yl, c),
            "mirror": flat(z, 1 - yh, x, 1 - yl, c),
            "core": flat(z, yh, x, yl, 1 - c),
        }[what]
        pairs.append((flat(z, yh, x, yl, c), to))
    return lax.ppermute(value, AXES, pairs)


def place():
    dp = lax.axis_index("dp")
    tensor = lax.axis_index("tensor")
    return dp // (YH * X), (dp // X) % YH, dp % X, tensor // CORE, tensor % CORE


def after(value, *earlier):
    return lax.optimization_barrier((value, *earlier))[0]


def gather_narrow(pair):
    return [pair, hop(pair, 0, 1), hop(pair, 0, -1), hop(pair, 0, 2)]


def gather_wide(narrow, earlier=()):
    top, bottom = jnp.concatenate(narrow[:2]), jnp.concatenate(narrow[2:])
    top, bottom = after(top, *earlier), after(bottom, *earlier)
    return [top, bottom, hop(top, 1, 1), hop(bottom, 1, 1), hop(top, 1, -1), hop(bottom, 1, -1)]


def gather_wide_whole(narrow, earlier=()):
    block = after(jnp.concatenate(narrow), *earlier)
    return [block, hop(block, 1, 1), hop(block, 1, -1)]


def gather_far(wide, *earlier):
    if len(wide) == 3:
        half = wide[0].shape[0] // 2
        plus, minus = after(wide[1][:half], *earlier), after(wide[2][half:], *earlier)
    else:
        plus, minus = after(wide[2], *earlier), after(wide[5], *earlier)
    return [*wide, hop(plus, 1, 1), hop(minus, 1, -1)]


def piece_rows():
    z, yh, x, _, c = place()
    rows = []
    for outer in SHIFTS:
        for inner in SHIFTS:
            for half in range(YH):
                px = (x + jnp.where(c == 0, inner, outer)) % X
                pz = (z + jnp.where(c == 0, outer, inner)) % Z
                rows.append(((pz * YH + (yh ^ half)) * X + px) * PIECE)
    return jnp.stack(rows).astype(jnp.int32)


def locate(sources, piece):
    for source in sources:
        held = source.shape[0] // PIECE
        if piece < held:
            return source, piece
        piece -= held


def project_body(transposed, rows_ref, place_ref, x_ref, *refs):
    *sources, out_ref, basis, total, sems = refs
    width, depth = basis.shape[1], basis.shape[0] // 4

    def start(chunk):
        for core in range(CORE):
            @pl.when(place_ref[1] == core)
            def _():
                for other in range(4):
                    outer, inner = (chunk, other) if core == 0 else (other, chunk)
                    for half in range(YH):
                        row = pl.multiple_of(rows_ref[outer * 8 + inner * 2 + half], PIECE)
                        source, piece = locate(sources, outer * 8 + inner * 2 + half)
                        pltpu.make_async_copy(
                            source.at[pl.ds(piece * PIECE, PIECE)],
                            basis.at[pl.ds(row, PIECE)],
                            sems.at[chunk],
                        ).start()

    def store(at, proj):
        if transposed:
            out_ref[at, :] = (proj * proj).T.astype(BF16)
        else:
            out_ref[:, at] = (proj * proj).astype(BF16)

    parts = [slice(left, min(left + 256, width)) for left in range(0, width, 256)]

    @pl.when(pl.program_id(0) == 0)
    def _():
        start(0)
        start(1)
        for chunk in range(4):
            pltpu.make_async_copy(basis.at[pl.ds(0, depth)], basis.at[pl.ds(0, depth)], sems.at[chunk]).wait()
            if chunk + 2 < 4:
                start(chunk + 2)
            rows = pl.ds(pl.multiple_of(place_ref[2 + chunk], depth), depth)
            for at in parts:
                proj = jnp.dot(x_ref[:, rows], basis[rows, at], preferred_element_type=F32)
                if chunk > 0:
                    proj += total[:, at]
                if chunk < 3:
                    total[:, at] = proj
                else:
                    store(at, proj)

    @pl.when(pl.program_id(0) > 0)
    def _():
        for at in parts:
            store(at, jnp.dot(x_ref[...], basis[:, at], preferred_element_type=F32))


def project_cost(tokens, depth, width):
    return pl.CostEstimate(
        flops=2 * tokens * depth * width // 20,
        bytes_accessed=2 * (tokens * depth + depth * width + tokens * width) // 20,
        transcendentals=0,
    )


def chunk_table(shard, depth):
    z, _, _, _, c = place()
    table = [shard * 4, c, *(((z + shift) % Z) * (depth // Z) for shift in SHIFTS)]
    return jnp.stack([jnp.asarray(v) for v in table]).astype(jnp.int32)


def project_square(x, first, tokens, rows, sources, transposed):
    depth = x.shape[1]
    width = sources[0].shape[1]
    step = 256
    if transposed:
        out_shape = jax.ShapeDtypeStruct((width, tokens), BF16)
        out_spec = pl.BlockSpec((width, step), lambda i, rows, first: (0, i))
    else:
        out_shape = jax.ShapeDtypeStruct((tokens, width), BF16)
        out_spec = pl.BlockSpec((step, width), lambda i, rows, first: (i, 0))
    return pl.pallas_call(
        functools.partial(project_body, transposed),
        out_shape=out_shape,
        grid_spec=pltpu.PrefetchScalarGridSpec(
            num_scalar_prefetch=2,
            grid=(tokens // step,),
            in_specs=[pl.BlockSpec((step, depth), lambda i, rows, first: (first[0] + i, 0))]
            + [pl.BlockSpec(memory_space=pl.ANY)] * len(sources),
            out_specs=out_spec,
            scratch_shapes=[
                pltpu.VMEM((depth, width), BF16),
                pltpu.VMEM((step, width), F32),
                pltpu.SemaphoreType.DMA((4,)),
            ],
        ),
        compiler_params=pltpu.CompilerParams(
            vmem_limit_bytes=VMEM, dimension_semantics=("arbitrary",)
        ),
        cost_estimate=project_cost(tokens, depth, width),
    )(rows, first, x, *sources)


def exponent_of(biggest):
    return jnp.clip(jnp.floor(jnp.log2(biggest)) - 14.0, -100.0, 120.0)


def encode(value, inverse):
    scaled = value * inverse
    second = scaled * scaled
    fourth = second * second
    power = fourth * fourth
    near = power.astype(BF16).astype(F32)
    return jnp.where(power < near, -near, near).astype(BF16)


def decode(code, scale):
    code = code.astype(F32)
    size = jnp.abs(code)
    power = size + code * (0.72 / 512)
    value = jnp.exp2(jnp.log2(power) * 0.125) * scale
    return jnp.where(size > 0.0, value, 0.0)


def message_scale(ref, rows):
    return jnp.exp2(ref[rows : rows + TILE, :].astype(F32)[0:1, 0:1])


def correct_body(where_ref, *refs):
    parts, squares, outs = refs[:8], refs[8:10], refs[10:14]
    held_parts, held_squares, total, own, codes, sems = refs[14:]
    part, width = own.shape
    loads = []
    for side in range(2):
        loads.append(pltpu.make_async_copy(squares[side], held_squares.at[side], sems.at[5 * side]))
        for n in range(4):
            source = parts[side * 4 + n]
            if source.shape[0] > part:
                source = source.at[pl.ds(pl.multiple_of(where_ref[20], part), part)]
            rows = pl.ds(pl.multiple_of(where_ref[n], part), part)
            loads.append(pltpu.make_async_copy(source, held_parts.at[side, rows], sems.at[5 * side + 1 + n]))
    for load in loads:
        load.start()
    biggest = jnp.zeros((1, 1), F32)
    for side in range(2):
        for load in loads[5 * side : 5 * side + 5]:
            load.wait()
        for low in range(0, width, 256):
            at = slice(low, min(low + 256, width))
            block = jnp.dot(held_parts[side], held_squares[side, :, at], preferred_element_type=F32)
            if side == 1:
                block += total[:, at]
                biggest = jnp.maximum(biggest, jnp.max(block, axis=(0, 1), keepdims=True))
            total[:, at] = block
    exponent = exponent_of(biggest)
    inverse = jnp.exp2(-exponent)
    stores = []
    for dest in (3, 1, 2, 0):
        for sub in range(4):
            row = pl.multiple_of(where_ref[4 + dest * 4 + sub], OWN)
            block = total[pl.ds(row, OWN), :]
            at = slice(sub * OWN, (sub + 1) * OWN)
            if dest == 0:
                own[at, :] = block
            else:
                codes[dest - 1, at, :] = encode(block, inverse)
        if dest > 0:
            codes[dest - 1, 4 * OWN :, :] = jnp.broadcast_to(exponent, (TILE, width)).astype(BF16)
        source = own if dest == 0 else codes.at[dest - 1]
        stores.append(pltpu.make_async_copy(source, outs[dest], sems.at[10 + dest]))
        stores[-1].start()
    for store in stores:
        store.wait()


def full(shape):
    return pl.BlockSpec(shape, lambda *_: (0,) * len(shape))


def correct(near, far, sq_near, sq_far, where):
    tokens, width = sq_near.shape
    rows = 4 * OWN
    shapes = [((rows, width), F32)] + [((rows + TILE, width), BF16)] * 3
    return pl.pallas_call(
        correct_body,
        out_shape=[jax.ShapeDtypeStruct(*s) for s in shapes],
        grid_spec=pltpu.PrefetchScalarGridSpec(
            num_scalar_prefetch=1,
            grid=(1,),
            in_specs=[pl.BlockSpec(memory_space=pl.ANY)] * 10,
            out_specs=[pl.BlockSpec(memory_space=pl.ANY)] * 4,
            scratch_shapes=[
                pltpu.VMEM((2, 4 * rows, tokens), BF16),
                pltpu.VMEM((2, tokens, width), BF16),
                pltpu.VMEM((4 * rows, width), F32),
                pltpu.VMEM((rows, width), F32),
                pltpu.VMEM((3, rows + TILE, width), BF16),
                pltpu.SemaphoreType.DMA((14,)),
            ],
        ),
        compiler_params=pltpu.CompilerParams(vmem_limit_bytes=VMEM),
        cost_estimate=pl.CostEstimate(flops=rows * tokens * width, bytes_accessed=rows * tokens, transcendentals=0),
    )(where, *near, *far, sq_near, sq_far)


def add_body(where_ref, own_ref, plus_ref, minus_ref, away_ref, *refs):
    outs, total = refs[:4], refs[4]
    rows, width = own_ref.shape
    messages = (plus_ref, minus_ref, away_ref)
    scales = [message_scale(ref, rows) for ref in messages]
    biggest = jnp.zeros((1, 1), F32)
    for top in range(0, rows, OWN):
        at = slice(top, top + OWN)
        block = own_ref[at, :]
        for ref, scale in zip(messages, scales):
            block = block + decode(ref[at, :], scale)
        total[at, :] = block
        biggest = jnp.maximum(biggest, jnp.max(block, axis=(0, 1), keepdims=True))
    exponent = exponent_of(biggest)
    inverse = jnp.exp2(-exponent)
    for n, out_ref in enumerate(outs):
        block = total[pl.ds(pl.multiple_of(where_ref[n], OWN), OWN), :]
        if out_ref.shape[0] == OWN:
            out_ref[...] = block
        else:
            out_ref[:OWN, :] = encode(block, inverse)
            out_ref[OWN:, :] = jnp.broadcast_to(exponent, (TILE, width)).astype(BF16)


def add(own, messages, where, keep):
    rows, width = own.shape
    shapes = [((OWN, width), F32) if keep else ((OWN + TILE, width), BF16)] + [((OWN + TILE, width), BF16)] * 3
    return pl.pallas_call(
        add_body,
        out_shape=[jax.ShapeDtypeStruct(*s) for s in shapes],
        grid_spec=pltpu.PrefetchScalarGridSpec(
            num_scalar_prefetch=1,
            grid=(1,),
            in_specs=[full((rows, width))] + [full((rows + TILE, width))] * 3,
            out_specs=[full(s[0]) for s in shapes],
            scratch_shapes=[pltpu.VMEM((rows, width), F32)],
        ),
        compiler_params=pltpu.CompilerParams(vmem_limit_bytes=VMEM),
        cost_estimate=pl.CostEstimate(flops=rows * width, bytes_accessed=rows * width, transcendentals=0),
    )(where, own, *messages)


def finish_body(factor, where_ref, own_ref, *refs):
    codes, out_ref = refs[:7], refs[7]
    width = own_ref.shape[1]
    for side in range(YH):
        total = own_ref[...] if side == 0 else jnp.zeros((OWN, width), F32)
        for ref in codes[3 * side : 3 + 4 * side]:
            total = total + decode(ref[:OWN, :], message_scale(ref, OWN))
        out_ref[:, pl.ds(pl.multiple_of(where_ref[side], width), width)] = total * factor


def finish(own, codes, where, factor):
    width = own.shape[1]
    return pl.pallas_call(
        functools.partial(finish_body, factor),
        out_shape=jax.ShapeDtypeStruct((OWN, YH * width), F32),
        grid_spec=pltpu.PrefetchScalarGridSpec(
            num_scalar_prefetch=1,
            grid=(1,),
            in_specs=[full(own.shape)] + [full((OWN + TILE, width))] * 7,
            out_specs=full((OWN, YH * width)),
        ),
        compiler_params=pltpu.CompilerParams(vmem_limit_bytes=VMEM),
        cost_estimate=pl.CostEstimate(flops=OWN * width, bytes_accessed=OWN * width, transcendentals=0),
    )(where, own, *codes)


def tables(flip):
    z, yh, x, yl, c = place()
    tensor = yl * CORE + c
    rows = 4 * OWN
    first = [t * rows for t in (tensor, tensor ^ 2, tensor ^ 1, tensor ^ 3)]
    for shift in (0, 1, -1, 2):
        for q in range(4):
            first.append(jnp.where(c == 0, q * rows + (x + shift) % X * OWN, (z + shift) % Z * rows + q * OWN))
    first.append((yh ^ flip) * rows)
    mine = jnp.where(c == 0, z, x)
    second = [(mine + shift) % 4 * OWN for shift in (0, 1, -1, 2)]
    return [jnp.stack([jnp.asarray(v) for v in t]).astype(jnp.int32) for t in (first, second)]


def share_tokens(acts):
    _, _, _, yl, c = place()
    quarter = acts.shape[0] // 4
    mine = lax.dynamic_slice(acts, ((yl * CORE + c) * quarter, 0), (quarter, acts.shape[1]))
    lines = [
        [flat(z, yh, x, yl, c) for yh in range(YH) for yl in range(YL) for c in range(CORE)]
        for z in range(Z)
        for x in range(X)
    ]
    return lax.all_gather(mine, AXES, axis_index_groups=lines, axis=0, tiled=True)


def on_device(acts, grads, eig_a, eig_g, total_tokens):
    _, yh, _, _, _ = place()
    half = eig_a.shape[1] // 2
    low, high = eig_a[:, :half], eig_a[:, half:]
    split = eig_g.shape[1]
    line = share_tokens(acts)
    tokens = acts.shape[0]
    rows = piece_rows()
    shard_near, shard_far = chunk_table(jnp.int32(0), acts.shape[1]), chunk_table(1 - yh, acts.shape[1])
    first_given, second = tables(1)
    first_kept, _ = tables(0)
    columns = jnp.stack([yh, 1 - yh]).astype(jnp.int32) * half

    other = swap(jnp.concatenate([eig_g, jnp.where(yh == 0, high, low)], axis=1), "yh")
    pair = jnp.concatenate([jnp.concatenate([eig_g, jnp.where(yh == 0, low, high)], axis=1), other])
    narrow = gather_narrow(pair)
    narrow[0] = after(narrow[0], rows, shard_near, shard_far, first_given, first_kept, second, columns)
    wide_g = gather_wide([v[:, :split] for v in narrow])
    basis_g = gather_far(wide_g)
    wide_a = gather_wide_whole([v[:, split:] for v in narrow], (wide_g[2], wide_g[5]))
    own_g = project_square(grads, shard_near, tokens, rows, basis_g, True)
    own_g_other_core = swap(own_g, "core")
    basis_a = gather_far(wide_a, own_g_other_core)
    sq_near = project_square(acts, shard_near, tokens, rows, basis_a, False)
    sq_far = project_square(line, shard_far, tokens, rows, basis_a, False)
    rows = own_g.shape[0] // 2
    given = lax.dynamic_slice(own_g, ((1 - yh) * rows, 0), (rows, tokens))
    kept = lax.dynamic_slice(own_g, (yh * rows, 0), (rows, tokens))
    beside_given, across_kept = swap(given, "yl"), swap(kept, "mirror")
    beside_given, across_kept = after(beside_given, sq_near), after(across_kept, sq_near)
    diagonal_kept = swap(across_kept, "yl")
    kept, given, beside = after(kept, across_kept), after(given, beside_given), beside_given
    beside_kept, across_given = swap(kept, "yl"), swap(given, "mirror")
    diagonal_given = swap(beside, "mirror")

    diagonal_kept = after(diagonal_kept, sq_far, across_given)
    near = [own_g, beside_given, own_g_other_core, swap(beside_given, "core")]
    far = [diagonal_kept, across_kept, swap(diagonal_kept, "core"), swap(across_kept, "core")]
    shifts = (1, -1, 2)
    own, *messages = correct(near, far, sq_near, sq_far, first_given)
    beside_kept, diagonal_given = after(beside_kept, own), after(diagonal_given, own)
    near = [own_g, beside_kept, own_g_other_core, swap(beside_kept, "core")]
    far = [diagonal_given, across_given, swap(diagonal_given, "core"), swap(across_given, "core")]
    received = [hop(message, 0, shift) for message, shift in zip(messages, shifts)]
    kept_own, *kept_messages = correct(near, far, sq_near, sq_far, first_kept)
    given_codes = add(after(own, kept_own), received, second, False)
    kept_messages = [after(message, *received) for message in kept_messages]
    received = [hop(message, 0, shift) for message, shift in zip(kept_messages, shifts)]
    given_codes = [hop(code, 1, shift, 1) for code, shift in zip(given_codes, (0, *shifts))]
    own, *codes = add(kept_own, received, second, True)
    codes = [hop(code, 1, shift) for code, shift in zip(codes, shifts)]
    return finish(own, codes + given_codes, columns, 1.0 / total_tokens)


def solution(mesh):
    placed = (P("dp", None), P("dp", None), P("dp", "tensor"), P("dp", "tensor"))
    body = functools.partial(on_device, total_tokens=32768)
    return jax.shard_map(body, mesh=mesh, in_specs=placed, out_specs=P("dp", "tensor"), check_vma=False)
```

```python
import functools

import jax
import jax.numpy as jnp
from jax import lax
from jax.experimental import pallas as pl
from jax.experimental.pallas import tpu as pltpu
from jax.sharding import PartitionSpec as P

AXES = ("dp", "tensor")
Z, YH, X, YL, CORE = 4, 2, 4, 2, 2
PIECE = 160
OWN = 80
TILE = 16
SHIFTS = (0, -1, 1, 2)
VMEM = 60 << 20
F32, BF16 = jnp.float32, jnp.bfloat16


def flat(z, yh, x, yl, c):
    return (((z * YH + yh) * X + x) * YL + yl) * CORE + c


def every():
    for z in range(Z):
        for yh in range(YH):
            for x in range(X):
                for yl in range(YL):
                    for c in range(CORE):
                        yield z, yh, x, yl, c


def hop(value, phase, shift, flip=0):
    pairs = []
    for z, yh, x, yl, c in every():
        if (phase + c) % 2 == 0:
            to = flat(z, yh ^ flip, (x + shift) % X, yl, c)
        else:
            to = flat((z + shift) % Z, yh ^ flip, x, yl, c)
        pairs.append((flat(z, yh, x, yl, c), to))
    return lax.ppermute(value, AXES, pairs)


def swap(value, what):
    pairs = []
    for z, yh, x, yl, c in every():
        to = {
            "yh": flat(z, 1 - yh, x, yl, c),
            "yl": flat(z, yh, x, 1 - yl, c),
            "mirror": flat(z, 1 - yh, x, 1 - yl, c),
            "core": flat(z, yh, x, yl, 1 - c),
        }[what]
        pairs.append((flat(z, yh, x, yl, c), to))
    return lax.ppermute(value, AXES, pairs)


def place():
    dp = lax.axis_index("dp")
    tensor = lax.axis_index("tensor")
    return dp // (YH * X), (dp // X) % YH, dp % X, tensor // CORE, tensor % CORE


def after(value, *earlier):
    return lax.optimization_barrier((value, *earlier))[0]


def gather_narrow(pair):
    return [pair, hop(pair, 0, 1), hop(pair, 0, -1), hop(pair, 0, 2)]


def gather_wide(narrow, earlier=()):
    top, bottom = jnp.concatenate(narrow[:2]), jnp.concatenate(narrow[2:])
    top, bottom = after(top, *earlier), after(bottom, *earlier)
    return [top, bottom, hop(top, 1, 1), hop(bottom, 1, 1), hop(top, 1, -1), hop(bottom, 1, -1)]


def gather_wide_whole(narrow, earlier=()):
    block = after(jnp.concatenate(narrow), *earlier)
    return [block, hop(block, 1, 1), hop(block, 1, -1)]


def gather_far(wide, *earlier):
    if len(wide) == 3:
        half = wide[0].shape[0] // 2
        plus, minus = after(wide[1][:half], *earlier), after(wide[2][half:], *earlier)
    else:
        plus, minus = after(wide[2], *earlier), after(wide[5], *earlier)
    return [*wide, hop(plus, 1, 1), hop(minus, 1, -1)]


def piece_rows():
    z, yh, x, _, c = place()
    rows = []
    for outer in SHIFTS:
        for inner in SHIFTS:
            for half in range(YH):
                px = (x + jnp.where(c == 0, inner, outer)) % X
                pz = (z + jnp.where(c == 0, outer, inner)) % Z
                rows.append(((pz * YH + (yh ^ half)) * X + px) * PIECE)
    return jnp.stack(rows).astype(jnp.int32)


def locate(sources, piece):
    for source in sources:
        held = source.shape[0] // PIECE
        if piece < held:
            return source, piece
        piece -= held


def project_body(transposed, rows_ref, place_ref, x_ref, *refs):
    *sources, out_ref, basis, total, sems = refs
    width, depth = basis.shape[1], basis.shape[0] // 4

    def start(chunk):
        for core in range(CORE):
            @pl.when(place_ref[1] == core)
            def _():
                for other in range(4):
                    outer, inner = (chunk, other) if core == 0 else (other, chunk)
                    for half in range(YH):
                        row = pl.multiple_of(rows_ref[outer * 8 + inner * 2 + half], PIECE)
                        source, piece = locate(sources, outer * 8 + inner * 2 + half)
                        pltpu.make_async_copy(
                            source.at[pl.ds(piece * PIECE, PIECE)],
                            basis.at[pl.ds(row, PIECE)],
                            sems.at[chunk],
                        ).start()

    def store(at, proj):
        if transposed:
            out_ref[at, :] = (proj * proj).T.astype(BF16)
        else:
            out_ref[:, at] = (proj * proj).astype(BF16)

    parts = [slice(left, min(left + 256, width)) for left in range(0, width, 256)]

    @pl.when(pl.program_id(0) == 0)
    def _():
        start(0)
        start(1)
        for chunk in range(4):
            pltpu.make_async_copy(basis.at[pl.ds(0, depth)], basis.at[pl.ds(0, depth)], sems.at[chunk]).wait()
            if chunk + 2 < 4:
                start(chunk + 2)
            rows = pl.ds(pl.multiple_of(place_ref[2 + chunk], depth), depth)
            for at in parts:
                proj = jnp.dot(x_ref[:, rows], basis[rows, at], preferred_element_type=F32)
                if chunk > 0:
                    proj += total[:, at]
                if chunk < 3:
                    total[:, at] = proj
                else:
                    store(at, proj)

    @pl.when(pl.program_id(0) > 0)
    def _():
        for at in parts:
            store(at, jnp.dot(x_ref[...], basis[:, at], preferred_element_type=F32))


def project_cost(tokens, depth, width):
    return pl.CostEstimate(
        flops=2 * tokens * depth * width // 20,
        bytes_accessed=2 * (tokens * depth + depth * width + tokens * width) // 20,
        transcendentals=0,
    )


def chunk_table(shard, depth):
    z, _, _, _, c = place()
    table = [shard * 4, c, *(((z + shift) % Z) * (depth // Z) for shift in SHIFTS)]
    return jnp.stack([jnp.asarray(v) for v in table]).astype(jnp.int32)


def project_square(x, first, tokens, rows, sources, transposed):
    depth = x.shape[1]
    width = sources[0].shape[1]
    step = 256
    if transposed:
        out_shape = jax.ShapeDtypeStruct((width, tokens), BF16)
        out_spec = pl.BlockSpec((width, step), lambda i, rows, first: (0, i))
    else:
        out_shape = jax.ShapeDtypeStruct((tokens, width), BF16)
        out_spec = pl.BlockSpec((step, width), lambda i, rows, first: (i, 0))
    return pl.pallas_call(
        functools.partial(project_body, transposed),
        out_shape=out_shape,
        grid_spec=pltpu.PrefetchScalarGridSpec(
            num_scalar_prefetch=2,
            grid=(tokens // step,),
            in_specs=[pl.BlockSpec((step, depth), lambda i, rows, first: (first[0] + i, 0))]
            + [pl.BlockSpec(memory_space=pl.ANY)] * len(sources),
            out_specs=out_spec,
            scratch_shapes=[
                pltpu.VMEM((depth, width), BF16),
                pltpu.VMEM((step, width), F32),
                pltpu.SemaphoreType.DMA((4,)),
            ],
        ),
        compiler_params=pltpu.CompilerParams(
            vmem_limit_bytes=VMEM, dimension_semantics=("arbitrary",)
        ),
        cost_estimate=project_cost(tokens, depth, width),
    )(rows, first, x, *sources)


def exponent_of(biggest):
    return jnp.clip(jnp.floor(jnp.log2(biggest)) - 14.0, -100.0, 120.0)


def encode(value, inverse):
    scaled = value * inverse
    second = scaled * scaled
    fourth = second * second
    power = fourth * fourth
    near = power.astype(BF16).astype(F32)
    return jnp.where(power < near, -near, near).astype(BF16)


def decode(code, scale):
    code = code.astype(F32)
    size = jnp.abs(code)
    power = size + code * (0.72 / 512)
    value = jnp.exp2(jnp.log2(power) * 0.125) * scale
    return jnp.where(size > 0.0, value, 0.0)


def message_scale(ref, rows):
    return jnp.exp2(ref[rows : rows + TILE, :].astype(F32)[0:1, 0:1])


def correct_body(where_ref, *refs):
    parts, squares, outs = refs[:8], refs[8:10], refs[10:14]
    held_parts, held_squares, total, own, codes, sems = refs[14:]
    part, width = own.shape
    tokens = squares[0].shape[0]
    loads = []
    for side in range(2):
        loads.append(
            pltpu.make_async_copy(squares[side], held_squares.at[pl.ds(side * tokens, tokens)], sems.at[5 * side])
        )
        for n in range(4):
            source = parts[side * 4 + n]
            if source.shape[0] > part:
                source = source.at[pl.ds(pl.multiple_of(where_ref[20], part), part)]
            rows = pl.ds(pl.multiple_of(where_ref[n], part), part)
            span = pl.ds(side * tokens, tokens)
            loads.append(pltpu.make_async_copy(source, held_parts.at[rows, span], sems.at[5 * side + 1 + n]))
    for load in loads:
        load.start()
    for load in loads:
        load.wait()
    biggest = jnp.zeros((1, 1), F32)
    for low in range(0, width, 256):
        at = slice(low, min(low + 256, width))
        block = jnp.dot(held_parts[...], held_squares[:, at], preferred_element_type=F32)
        biggest = jnp.maximum(biggest, jnp.max(block, axis=(0, 1), keepdims=True))
        total[:, at] = block
    exponent = exponent_of(biggest)
    inverse = jnp.exp2(-exponent)
    stores = []
    for dest in (3, 1, 2, 0):
        for sub in range(4):
            row = pl.multiple_of(where_ref[4 + dest * 4 + sub], OWN)
            block = total[pl.ds(row, OWN), :]
            at = slice(sub * OWN, (sub + 1) * OWN)
            if dest == 0:
                own[at, :] = block
            else:
                codes[dest - 1, at, :] = encode(block, inverse)
        if dest > 0:
            codes[dest - 1, 4 * OWN :, :] = jnp.broadcast_to(exponent, (TILE, width)).astype(BF16)
        source = own if dest == 0 else codes.at[dest - 1]
        stores.append(pltpu.make_async_copy(source, outs[dest], sems.at[10 + dest]))
        stores[-1].start()
    for store in stores:
        store.wait()


def full(shape):
    return pl.BlockSpec(shape, lambda *_: (0,) * len(shape))


def correct(near, far, sq_near, sq_far, where):
    tokens, width = sq_near.shape
    rows = 4 * OWN
    shapes = [((rows, width), F32)] + [((rows + TILE, width), BF16)] * 3
    return pl.pallas_call(
        correct_body,
        out_shape=[jax.ShapeDtypeStruct(*s) for s in shapes],
        grid_spec=pltpu.PrefetchScalarGridSpec(
            num_scalar_prefetch=1,
            grid=(1,),
            in_specs=[pl.BlockSpec(memory_space=pl.ANY)] * 10,
            out_specs=[pl.BlockSpec(memory_space=pl.ANY)] * 4,
            scratch_shapes=[
                pltpu.VMEM((4 * rows, 2 * tokens), BF16),
                pltpu.VMEM((2 * tokens, width), BF16),
                pltpu.VMEM((4 * rows, width), F32),
                pltpu.VMEM((rows, width), F32),
                pltpu.VMEM((3, rows + TILE, width), BF16),
                pltpu.SemaphoreType.DMA((14,)),
            ],
        ),
        compiler_params=pltpu.CompilerParams(vmem_limit_bytes=VMEM),
        cost_estimate=pl.CostEstimate(flops=rows * tokens * width, bytes_accessed=rows * tokens, transcendentals=0),
    )(where, *near, *far, sq_near, sq_far)


def add_body(where_ref, own_ref, plus_ref, minus_ref, away_ref, *refs):
    outs, total = refs[:4], refs[4]
    rows, width = own_ref.shape
    messages = (plus_ref, minus_ref, away_ref)
    scales = [message_scale(ref, rows) for ref in messages]
    biggest = jnp.zeros((1, 1), F32)
    for top in range(0, rows, OWN):
        at = slice(top, top + OWN)
        block = own_ref[at, :]
        for ref, scale in zip(messages, scales):
            block = block + decode(ref[at, :], scale)
        total[at, :] = block
        biggest = jnp.maximum(biggest, jnp.max(block, axis=(0, 1), keepdims=True))
    exponent = exponent_of(biggest)
    inverse = jnp.exp2(-exponent)
    for n, out_ref in enumerate(outs):
        block = total[pl.ds(pl.multiple_of(where_ref[n], OWN), OWN), :]
        if out_ref.shape[0] == OWN:
            out_ref[...] = block
        else:
            out_ref[:OWN, :] = encode(block, inverse)
            out_ref[OWN:, :] = jnp.broadcast_to(exponent, (TILE, width)).astype(BF16)


def add(own, messages, where, keep):
    rows, width = own.shape
    shapes = [((OWN, width), F32) if keep else ((OWN + TILE, width), BF16)] + [((OWN + TILE, width), BF16)] * 3
    return pl.pallas_call(
        add_body,
        out_shape=[jax.ShapeDtypeStruct(*s) for s in shapes],
        grid_spec=pltpu.PrefetchScalarGridSpec(
            num_scalar_prefetch=1,
            grid=(1,),
            in_specs=[full((rows, width))] + [full((rows + TILE, width))] * 3,
            out_specs=[full(s[0]) for s in shapes],
            scratch_shapes=[pltpu.VMEM((rows, width), F32)],
        ),
        compiler_params=pltpu.CompilerParams(vmem_limit_bytes=VMEM),
        cost_estimate=pl.CostEstimate(flops=rows * width, bytes_accessed=rows * width, transcendentals=0),
    )(where, own, *messages)


def finish_body(factor, where_ref, own_ref, *refs):
    codes, out_ref = refs[:7], refs[7]
    width = own_ref.shape[1]
    for side in range(YH):
        total = own_ref[...] if side == 0 else jnp.zeros((OWN, width), F32)
        for ref in codes[3 * side : 3 + 4 * side]:
            total = total + decode(ref[:OWN, :], message_scale(ref, OWN))
        out_ref[:, pl.ds(pl.multiple_of(where_ref[side], width), width)] = total * factor


def finish(own, codes, where, factor):
    width = own.shape[1]
    return pl.pallas_call(
        functools.partial(finish_body, factor),
        out_shape=jax.ShapeDtypeStruct((OWN, YH * width), F32),
        grid_spec=pltpu.PrefetchScalarGridSpec(
            num_scalar_prefetch=1,
            grid=(1,),
            in_specs=[full(own.shape)] + [full((OWN + TILE, width))] * 7,
            out_specs=full((OWN, YH * width)),
        ),
        compiler_params=pltpu.CompilerParams(vmem_limit_bytes=VMEM),
        cost_estimate=pl.CostEstimate(flops=OWN * width, bytes_accessed=OWN * width, transcendentals=0),
    )(where, own, *codes)


def tables(flip):
    z, yh, x, yl, c = place()
    tensor = yl * CORE + c
    rows = 4 * OWN
    first = [t * rows for t in (tensor, tensor ^ 2, tensor ^ 1, tensor ^ 3)]
    for shift in (0, 1, -1, 2):
        for q in range(4):
            first.append(jnp.where(c == 0, q * rows + (x + shift) % X * OWN, (z + shift) % Z * rows + q * OWN))
    first.append((yh ^ flip) * rows)
    mine = jnp.where(c == 0, z, x)
    second = [(mine + shift) % 4 * OWN for shift in (0, 1, -1, 2)]
    return [jnp.stack([jnp.asarray(v) for v in t]).astype(jnp.int32) for t in (first, second)]


def share_tokens(acts):
    _, _, _, yl, c = place()
    quarter = acts.shape[0] // 4
    mine = lax.dynamic_slice(acts, ((yl * CORE + c) * quarter, 0), (quarter, acts.shape[1]))
    lines = [
        [flat(z, yh, x, yl, c) for yh in range(YH) for yl in range(YL) for c in range(CORE)]
        for z in range(Z)
        for x in range(X)
    ]
    return lax.all_gather(mine, AXES, axis_index_groups=lines, axis=0, tiled=True)


def on_device(acts, grads, eig_a, eig_g, total_tokens):
    _, yh, _, _, _ = place()
    half = eig_a.shape[1] // 2
    low, high = eig_a[:, :half], eig_a[:, half:]
    split = eig_g.shape[1]
    line = share_tokens(acts)
    tokens = acts.shape[0]
    rows = piece_rows()
    shard_near, shard_far = chunk_table(jnp.int32(0), acts.shape[1]), chunk_table(1 - yh, acts.shape[1])
    first_given, second = tables(1)
    first_kept, _ = tables(0)
    columns = jnp.stack([yh, 1 - yh]).astype(jnp.int32) * half

    other = swap(jnp.concatenate([eig_g, jnp.where(yh == 0, high, low)], axis=1), "yh")
    pair = jnp.concatenate([jnp.concatenate([eig_g, jnp.where(yh == 0, low, high)], axis=1), other])
    narrow = gather_narrow(pair)
    narrow[0] = after(narrow[0], rows, shard_near, shard_far, first_given, first_kept, second, columns)
    wide_g = gather_wide([v[:, :split] for v in narrow])
    basis_g = gather_far(wide_g)
    wide_a = gather_wide_whole([v[:, split:] for v in narrow], (wide_g[2], wide_g[5]))
    own_g = project_square(grads, shard_near, tokens, rows, basis_g, True)
    own_g_other_core = swap(own_g, "core")
    basis_a = gather_far(wide_a, own_g_other_core)
    sq_near = project_square(acts, shard_near, tokens, rows, basis_a, False)
    sq_far = project_square(line, shard_far, tokens, rows, basis_a, False)
    rows = own_g.shape[0] // 2
    given = lax.dynamic_slice(own_g, ((1 - yh) * rows, 0), (rows, tokens))
    kept = lax.dynamic_slice(own_g, (yh * rows, 0), (rows, tokens))
    beside_given, across_kept = swap(given, "yl"), swap(kept, "mirror")
    beside_given, across_kept = after(beside_given, sq_near), after(across_kept, sq_near)
    diagonal_kept = swap(across_kept, "yl")
    kept, given, beside = after(kept, across_kept), after(given, beside_given), beside_given
    beside_kept, across_given = swap(kept, "yl"), swap(given, "mirror")
    diagonal_given = swap(beside, "mirror")

    diagonal_kept = after(diagonal_kept, sq_far, across_given)
    near = [own_g, beside_given, own_g_other_core, swap(beside_given, "core")]
    far = [diagonal_kept, across_kept, swap(diagonal_kept, "core"), swap(across_kept, "core")]
    shifts = (1, -1, 2)
    own, *messages = correct(near, far, sq_near, sq_far, first_given)
    beside_kept, diagonal_given = after(beside_kept, own), after(diagonal_given, own)
    near = [own_g, beside_kept, own_g_other_core, swap(beside_kept, "core")]
    far = [diagonal_given, across_given, swap(diagonal_given, "core"), swap(across_given, "core")]
    received = [hop(message, 0, shift) for message, shift in zip(messages, shifts)]
    kept_own, *kept_messages = correct(near, far, sq_near, sq_far, first_kept)
    given_codes = add(after(own, kept_own), received, second, False)
    kept_messages = [after(message, *received) for message in kept_messages]
    received = [hop(message, 0, shift) for message, shift in zip(kept_messages, shifts)]
    given_codes = [hop(code, 1, shift, 1) for code, shift in zip(given_codes, (0, *shifts))]
    own, *codes = add(kept_own, received, second, True)
    codes = [hop(code, 1, shift) for code, shift in zip(codes, shifts)]
    return finish(own, codes + given_codes, columns, 1.0 / total_tokens)


def solution(mesh):
    placed = (P("dp", None), P("dp", None), P("dp", "tensor"), P("dp", "tensor"))
    body = functools.partial(on_device, total_tokens=32768)
    return jax.shard_map(body, mesh=mesh, in_specs=placed, out_specs=P("dp", "tensor"), check_vma=False)
```
